256 devices in a mesh: morton: 32 (over z, y), tile: 8 (over x, core).
Axes of the slice: x: 4, y: 4, z: 8, core: 2. Of those that a mesh axis runs over, the one named last changes fastest.
Arguments:
- moments: bfloat16 [8192, 64, 128], P(('morton', 'tile')), may hold values from -6 to 6
- dipole_pos: bfloat16 [8192, 3, 128], P(('morton', 'tile')), as said below
- send_index: int32 [8192, 2], P(('morton', 'tile')), may hold values from 0 to 31, as said below
- send_count: int32 [8192], P(('morton', 'tile')), may hold values from 1 to 2, as said below
- reading_pos: bfloat16 [16384, 3, 128], P(('morton', 'tile')), as said below
- near_cols: int32 [16384, 16], P(('morton', 'tile')), may hold values from 0 to 63, as said below
- grid_slot: int32 [16384], P(('morton', 'tile')), may hold values from 0 to 511, as said below
- observed: bfloat16 [16384, 64, 128], P(('morton', 'tile')), may hold values from -6 to 6
Outputs:
- field: bfloat16 [16384, 64, 128], P(('morton', 'tile'))
- adjoint_moments: float32 [8192, 64, 128], P(('morton', 'tile'))
The draws below stay inside these ranges and needn't reach their ends.
Inputs may be any that keep to these rules, and one draw needn't show every extreme that they name: send_count has the value 2 at every row with q = p; the live entries of one leaf range's rows name every one of its 32 old blocks. `send_index`: entries past send_count are padding; live entries of the rows of leaf range g name old blocks 0 to 31 of g, each at least once. `near_cols`: every entry of the rows of leaf range g names a live slot of g, and every live slot of g is named at least once. `grid_slot`: for the reading blocks of leaf range g with tile index t, the values are d * 64 + t * 8 + e with each pair (d, e), d < 8, e < 8, taken once. `dipole_pos`: coordinates are multiples of 1/16; dipoles lie 0.5 or more below every reading. `reading_pos`: coordinates are multiples of 1/16.
All inputs are finite; a program needn't handle non-finite values.
Results may differ from the reference program's by a relative error of at most 0.005.
Values may be sent and summed in bfloat16 or wider, within the bound.
No kernel may reach another device: no remote copies, remote signals or barrier semaphores. Data moves between devices by JAX's collectives and lax.ppermute only.
A program may use at most 64 MiB of HBM per device.

```python
import jax
import jax.numpy as jnp
from jax import lax

COLS = 64
BLK = 128
NB = 16
CAP = 2
RB = 64
OLD = 32
READ_BLOCKS = 16384
DIP_BLOCKS = 8192
N_MORTON = 32
N_TILE = 8


def counts_table(key):
    table = jax.random.randint(jax.random.fold_in(key, 101), (N_MORTON, N_TILE, N_MORTON), 1, CAP + 1)
    same = jnp.arange(N_MORTON)[:, None, None] == jnp.arange(N_MORTON)[None, None, :]
    return jnp.where(same, CAP, table).astype(jnp.int32)


def draw_send_count(key, part):
    return counts_table(key).reshape(-1)


def draw_send_index(key, part):
    ranges = N_MORTON * N_TILE
    slots = N_MORTON * CAP
    counts = counts_table(key).reshape(ranges, N_MORTON)
    live = (jnp.arange(CAP)[None, None, :] < counts[:, :, None]).reshape(ranges, slots)
    ranks = jnp.cumsum(live.astype(jnp.int32), axis=1) - 1
    ranks = jnp.where(live, ranks, jnp.arange(slots, dtype=jnp.int32)[None, :])
    orders = jax.vmap(lambda k: jax.random.permutation(k, OLD))(jax.random.split(jax.random.fold_in(key, 202), ranges))
    picked = jnp.take_along_axis(orders, ranks % OLD, axis=1)
    return picked.reshape(ranges * N_MORTON, CAP).astype(jnp.int32)


def draw_near_cols(key, part):
    ranges = N_MORTON * N_TILE
    slots = N_MORTON * CAP
    counts = counts_table(key)
    received = jnp.transpose(counts, (2, 1, 0)).reshape(ranges, N_MORTON)
    live = (jnp.arange(CAP)[None, None, :] < received[:, :, None]).reshape(ranges, slots)
    slot_index_list = jnp.arange(slots, dtype=jnp.int32)
    order = jnp.argsort(jnp.where(live, slot_index_list[None, :], slot_index_list[None, :] + slots), axis=1)
    live_total = jnp.sum(live.astype(jnp.int32), axis=1)
    mixes = jax.vmap(lambda k: jax.random.permutation(k, RB * NB))(jax.random.split(jax.random.fold_in(key, 303), ranges))
    refs = jnp.take_along_axis(order, mixes % live_total[:, None], axis=1)
    return refs.reshape(ranges * RB, NB).astype(jnp.int32)


def draw_grid_slot(key, part):
    ranges = N_MORTON * N_TILE
    orders = jax.vmap(lambda k: jax.random.permutation(k, RB))(jax.random.split(jax.random.fold_in(key, 404), ranges))
    tiles = jnp.arange(ranges, dtype=jnp.int32) % N_TILE
    dest = orders % N_TILE
    inner = orders // N_TILE
    slot = dest * RB + tiles[:, None] * (RB // N_TILE) + inner
    return slot.reshape(-1).astype(jnp.int32)


def coordinates(key, rows, depth_lo, depth_levels):
    key_x, key_y, key_z = jax.random.split(key, 3)
    span = 128
    xs = jax.random.randint(key_x, (rows, BLK), 0, span).astype(jnp.float32) / 16.0
    ys = jax.random.randint(key_y, (rows, BLK), 0, span).astype(jnp.float32) / 16.0
    zs = depth_lo + jax.random.randint(key_z, (rows, BLK), 0, depth_levels).astype(jnp.float32) / 16.0
    return jnp.stack([xs, ys, zs], axis=1)


def draw_dipole_pos(key, part):
    rows = OLD * N_MORTON * N_TILE
    return coordinates(jax.random.fold_in(key, 505), rows, -1.4375, 16).astype(jnp.bfloat16)


def draw_reading_pos(key, part):
    rows = RB * N_MORTON * N_TILE
    return coordinates(jax.random.fold_in(key, 606), rows, 0.0, 8).astype(jnp.bfloat16)


def levels(own_key, extent, shards, low, high):
    level = 1.0
    for axis_at, blocks in shards:
        draws = jax.random.uniform(jax.random.fold_in(jax.random.fold_in(own_key, 6), axis_at), (blocks,), jnp.float32, low / len(shards), high / len(shards))
        level = level * jnp.repeat(jnp.exp(draws), extent[axis_at] // blocks).reshape((-1,) + (1,) * (len(extent) - 1 - axis_at))
    return level


def scatter_about(rng, shape, spread, bound, pieces=(), kind=jnp.bfloat16):
    values = jax.random.normal(rng, shape, jnp.float32) * spread
    if len(pieces) > 0:
        values = levels(rng, shape, pieces, -0.22, 0.18) * values
    return jnp.clip(values, min=-bound, max=bound).astype(kind)


def setup_inputs(seed: int = 0) -> dict:
    key_of = jax.random.split(jax.random.key(seed), 9)
    moments = scatter_about(key_of[0], (DIP_BLOCKS, COLS, BLK), 1.0, 6.0, ((0, 256),))
    dipole_pos = draw_dipole_pos(jax.random.fold_in(key_of[8], 71), 0)
    send_index = draw_send_index(jax.random.fold_in(key_of[8], 71), 0)
    send_count = draw_send_count(jax.random.fold_in(key_of[8], 71), 0)
    reading_pos = draw_reading_pos(jax.random.fold_in(key_of[8], 71), 0)
    near_cols = draw_near_cols(jax.random.fold_in(key_of[8], 71), 0)
    grid_slot = draw_grid_slot(jax.random.fold_in(key_of[8], 71), 0)
    observed = scatter_about(key_of[7], (READ_BLOCKS, COLS, BLK), 1.0, 6.0, ((0, 256),))
    return dict(moments=moments, dipole_pos=dipole_pos, send_index=send_index, send_count=send_count, reading_pos=reading_pos, near_cols=near_cols, grid_slot=grid_slot, observed=observed)


kernel_scale = 0.2

def kernel_blocks(read_one, dip_blocks):
    reads = read_one.astype(jnp.float32)
    dips = dip_blocks.astype(jnp.float32)
    offset_east = reads[0][None, None, :] - dips[:, 0, :, None]
    offset_north = reads[1][None, None, :] - dips[:, 1, :, None]
    offset_vertical = reads[2][None, None, :] - dips[:, 2, :, None]
    distance_squared = offset_east * offset_east + offset_north * offset_north + offset_vertical * offset_vertical
    kernel_values = kernel_scale * (2.0 * offset_vertical * offset_vertical - offset_east * offset_east - offset_north * offset_north) / (distance_squared * distance_squared * jnp.sqrt(distance_squared))
    return kernel_values.astype(jnp.bfloat16)

def forward_device(slot_m, slot_p, read_dev, col_dev):

    def one(items):
        read_one, cols_one = items
        kern = kernel_blocks(read_one, slot_p[cols_one])
        out = jnp.einsum('kcd,kdr->cr', slot_m[cols_one].astype(jnp.float32), kern.astype(jnp.float32))
        return out.astype(jnp.bfloat16)
    return lax.map(one, (read_dev, col_dev))

def adjoint_device(slot_p, read_dev, col_dev, res_dev, slots):

    def step(total, items):
        read_one, cols_one, res_one = items
        kern = kernel_blocks(read_one, slot_p[cols_one])
        contrib = jnp.einsum('cr,kdr->kcd', res_one.astype(jnp.float32), kern.astype(jnp.float32))
        return (total.at[cols_one].add(contrib), None)
    start = jnp.zeros((slots, COLS, BLK), jnp.float32)
    total, _ = lax.scan(step, start, (read_dev, col_dev, res_dev))
    return total

def reference(moments, dipole_pos, send_index, send_count, reading_pos, near_cols, grid_slot, observed):
    devs = N_MORTON * N_TILE
    slots = N_MORTON * CAP
    dev = jnp.arange(devs, dtype=jnp.int32)
    owner_row = dev // N_TILE
    tile_of = dev % N_TILE
    peers = jnp.arange(N_MORTON, dtype=jnp.int32)
    source = peers[None, :] * N_TILE + tile_of[:, None]
    rows = (source * N_MORTON + owner_row[:, None]).astype(jnp.int32)
    slot_block = (source[:, :, None] * OLD + send_index[rows]).reshape(devs, slots).astype(jnp.int32)
    live = (jnp.arange(CAP)[None, None, :] < send_count[rows][:, :, None]).reshape(devs, slots)
    reads = reading_pos.reshape(devs, RB, 3, BLK)
    cols = near_cols.reshape(devs, RB, NB)

    def forward_one(items):
        blocks, alive, read_dev, col_dev = items
        slot_m = jnp.where(alive[:, None, None], moments[blocks], jnp.zeros((), jnp.bfloat16))
        slot_p = dipole_pos[blocks]
        return forward_device(slot_m, slot_p, read_dev, col_dev)
    field_leaf = lax.map(forward_one, (slot_block, live, reads, cols)).reshape(devs * RB, COLS, BLK)
    group_start_index = jnp.arange(devs * RB, dtype=jnp.int32) // (N_TILE * RB) * (N_TILE * RB)
    place = (group_start_index + grid_slot).astype(jnp.int32)
    field = jnp.zeros_like(field_leaf).at[place].set(field_leaf)
    residual = (field.astype(jnp.float32) - observed.astype(jnp.float32)).astype(jnp.bfloat16)
    res_leaf = residual[place].reshape(devs, RB, COLS, BLK)

    def adjoint_one(total, items):
        blocks, alive, read_dev, col_dev, res_dev = items
        slot_p = dipole_pos[blocks]
        slot_adj = adjoint_device(slot_p, read_dev, col_dev, res_dev, slots)
        slot_adj = jnp.where(alive[:, None, None], slot_adj, jnp.zeros((), jnp.float32))
        return (total.at[blocks].add(slot_adj), None)
    start = jnp.zeros((devs * OLD, COLS, BLK), jnp.float32)
    adjoint_moments, _ = lax.scan(adjoint_one, start, (slot_block, live, reads, cols, res_leaf))
    return (field, adjoint_moments)
```

```python
import functools

import jax
import jax.numpy as jnp
from jax import lax
from jax.experimental import pallas as pl
from jax.experimental.pallas import tpu as pltpu
from jax.sharding import PartitionSpec as P

SHRINK = 0.6 ** (-1.0 / 3.0) / 2.0
UNDO = 0.125
GEN = 2
USE = 8
VMEM = 48 * 2**20


def make_kernels(cols_ref, pos_ref, read_ref, out_ref, read_wide):
    group, axes, blk = read_ref.shape
    near = out_ref.shape[2] // blk
    first = pl.program_id(0) * group
    for b in range(group):
        down = jnp.transpose(read_ref[b].astype(jnp.float32) * SHRINK)
        for c in range(axes):
            read_wide[b, c] = jnp.broadcast_to(down[:, c : c + 1], (blk, blk))

        def one(k, carry, b=b):
            p = pos_ref[cols_ref[first + b, k]].astype(jnp.float32) * SHRINK
            dx = read_wide[b, 0] - p[0:1]
            dy = read_wide[b, 1] - p[1:2]
            dz = read_wide[b, 2] - p[2:3]
            up = dz * dz
            inv = lax.rsqrt(dx * dx + dy * dy + up)
            inv2 = inv * inv
            value = (up * inv2 - (1.0 / 3.0)) * (inv2 * inv)
            out_ref[b, :, pl.ds(pl.multiple_of(k * blk, blk), blk)] = value.astype(out_ref.dtype)
            return carry

        lax.fori_loop(0, near, one, 0, unroll=2)


def kernel_values(near_cols, slot_p, reading_pos):
    rb, axes, blk = reading_pos.shape
    near = near_cols.shape[1]
    return pl.pallas_call(
        make_kernels,
        grid_spec=pltpu.PrefetchScalarGridSpec(
            num_scalar_prefetch=1,
            grid=(rb // GEN,),
            in_specs=[
                pl.BlockSpec(slot_p.shape, lambda g, *_: (0, 0, 0)),
                pl.BlockSpec((GEN, axes, blk), lambda g, *_: (g, 0, 0)),
            ],
            out_specs=pl.BlockSpec((GEN, blk, near * blk), lambda g, *_: (g, 0, 0)),
            scratch_shapes=[pltpu.VMEM((GEN, axes, blk, blk), jnp.float32)],
        ),
        out_shape=jax.ShapeDtypeStruct((rb, blk, near * blk), jnp.bfloat16),
        compiler_params=pltpu.CompilerParams(vmem_limit_bytes=VMEM),
        cost_estimate=pl.CostEstimate(
            flops=15 * rb * near * blk * blk,
            bytes_accessed=2 * rb * near * blk * blk,
            transcendentals=rb * near * blk * blk,
        ),
        name="kernel_values",
    )(near_cols, slot_p, reading_pos)


def apply_both(cols_ref, key_ref, kern_ref, m_ref, obs_ref, field_ref, adj_ref, m_wide, total):
    group, blk, wide = kern_ref.shape
    near = wide // blk
    step = pl.program_id(0)

    @pl.when(step == 0)
    def _():
        total[...] = jnp.zeros_like(total)

    for b in range(group):
        i = step * group + b
        at = key_ref[i]
        for k in range(near):
            m_wide[b, :, k * blk : (k + 1) * blk] = m_ref[cols_ref[i, k]]
        field = lax.dot_general(
            m_wide[b], kern_ref[b], (((1,), (1,)), ((), ())), preferred_element_type=jnp.float32
        )
        field = (field * UNDO).astype(jnp.bfloat16)
        field_ref[at] = field
        res = (field.astype(jnp.float32) - obs_ref[at].astype(jnp.float32)).astype(jnp.bfloat16)
        for k in range(near):
            total[cols_ref[i, k]] += jnp.dot(
                res, kern_ref[b, :, k * blk : (k + 1) * blk], preferred_element_type=jnp.float32
            )

    @pl.when(step == pl.num_programs(0) - 1)
    def _():
        adj_ref[...] = (total[...] * UNDO).astype(adj_ref.dtype)


def forward_adjoint(near_cols, order_key, kern, slot_m, observed):
    rb, blk, wide = kern.shape
    slots, width, _ = slot_m.shape
    whole = lambda g, *_: (0, 0, 0)
    return pl.pallas_call(
        apply_both,
        grid_spec=pltpu.PrefetchScalarGridSpec(
            num_scalar_prefetch=2,
            grid=(rb // USE,),
            in_specs=[
                pl.BlockSpec((USE, blk, wide), lambda g, *_: (g, 0, 0)),
                pl.BlockSpec(slot_m.shape, whole),
                pl.BlockSpec(observed.shape, whole),
            ],
            out_specs=[pl.BlockSpec((rb, width, blk), whole), pl.BlockSpec((slots, width, blk), whole)],
            scratch_shapes=[
                pltpu.VMEM((USE, width, wide), jnp.bfloat16),
                pltpu.VMEM((slots, width, blk), jnp.float32),
            ],
        ),
        out_shape=[
            jax.ShapeDtypeStruct((rb, width, blk), jnp.bfloat16),
            jax.ShapeDtypeStruct((slots, width, blk), jnp.bfloat16),
        ],
        compiler_params=pltpu.CompilerParams(vmem_limit_bytes=VMEM),
        cost_estimate=pl.CostEstimate(
            flops=4 * width * rb * wide * blk, bytes_accessed=2 * rb * wide * blk, transcendentals=0
        ),
        name="forward_adjoint",
    )(near_cols, order_key, kern, slot_m, observed)


def add_back(block_ref, live_ref, back_ref, out_ref):
    out_ref[...] = jnp.zeros_like(out_ref)

    def one(s, carry):
        alive = live_ref[s] > 0
        out_ref[block_ref[s]] += jnp.where(alive, back_ref[s].astype(jnp.float32), 0.0)
        return carry

    lax.fori_loop(0, back_ref.shape[0], one, 0, unroll=4)


def combine(flat_index, live, back, old):
    _, width, depth = back.shape
    return pl.pallas_call(
        add_back,
        grid_spec=pltpu.PrefetchScalarGridSpec(
            num_scalar_prefetch=2,
            grid=(1,),
            in_specs=[pl.BlockSpec(back.shape, lambda g, *_: (0, 0, 0))],
            out_specs=pl.BlockSpec((old, width, depth), lambda g, *_: (0, 0, 0)),
        ),
        out_shape=jax.ShapeDtypeStruct((old, width, depth), jnp.float32),
        compiler_params=pltpu.CompilerParams(vmem_limit_bytes=VMEM),
        name="combine",
    )(flat_index, live, back)


def on_device(
    moments, dipole_pos, send_index, send_count, reading_pos, near_cols, grid_slot, observed
):
    peers = lax.axis_size("morton")
    tiles = lax.axis_size("tile")
    cap = send_index.shape[1]
    old, width, depth = moments.shape
    rb = reading_pos.shape[0]
    share = rb // tiles
    swap = functools.partial(lax.all_to_all, split_axis=0, concat_axis=0, tiled=True)
    live = (jnp.arange(cap)[None, :] < send_count[:, None]).reshape(-1)
    flat_index = send_index.reshape(-1)
    send_p = dipole_pos[flat_index]
    slot_p = swap(send_p.reshape(peers, cap, 3, depth), "morton").reshape(peers * cap, 3, depth)
    send_m = jnp.where(live[:, None, None], moments[flat_index], jnp.zeros((), jnp.bfloat16))
    slot_m = swap(send_m.reshape(peers, cap, width, depth), "morton").reshape(
        peers * cap, width, depth
    )
    leaf_obs = swap(observed.reshape(tiles, share, width, depth), "tile").reshape(rb, width, depth)
    order_key = grid_slot // rb * share + grid_slot % rb % share
    kern = kernel_values(near_cols, slot_p, reading_pos)
    ordered, slot_adj = forward_adjoint(near_cols, order_key, kern, slot_m, leaf_obs)
    back = swap(slot_adj.reshape(peers, cap, width, depth), "morton").reshape(
        peers * cap, width, depth
    )
    field = swap(ordered.reshape(tiles, share, width, depth), "tile").reshape(rb, width, depth)
    adjoint_moments = combine(flat_index, live.astype(jnp.int32), back, old)
    return (field, adjoint_moments)


def solution(mesh):
    return jax.shard_map(
        on_device,
        mesh=mesh,
        in_specs=(
            P(("morton", "tile"), None, None),
            P(("morton", "tile"), None, None),
            P(("morton", "tile"), None),
            P(("morton", "tile")),
            P(("morton", "tile"), None, None),
            P(("morton", "tile"), None),
            P(("morton", "tile")),
            P(("morton", "tile"), None, None),
        ),
        out_specs=(P(("morton", "tile"), None, None), P(("morton", "tile"), None, None)),
        check_vma=False,
    )
```

```python
import functools

import jax
import jax.numpy as jnp
from jax import lax
from jax.experimental import pallas as pl
from jax.experimental.pallas import tpu as pltpu
from jax.sharding import PartitionSpec as P

SCALE = 0.2
REACH = 64.0
GEN = 8
USE = 8
ROWS = 16
VMEM = 50 * 2**20


def squares(p):
    blk = p.shape[1]
    x, y, z = (p[c : c + 1] * p[c : c + 1] for c in range(3))
    return jnp.broadcast_to(x + y + z, (8, blk)), jnp.broadcast_to(2.0 * z - x - y, (8, blk))


def pieces(value):
    high = value.astype(jnp.bfloat16).astype(jnp.float32)
    rest = value - high
    middle = rest.astype(jnp.bfloat16).astype(jnp.float32)
    return high, middle, rest - middle


def rows_of(table, shape):
    row = lax.broadcasted_iota(jnp.int32, shape, 0)
    out = jnp.zeros(shape, jnp.float32)
    for at, value in table.items():
        out = jnp.where(row == at, value, out)
    return out


def reading_features(read_ref, feat_ref):
    for b in range(read_ref.shape[0]):
        p = read_ref[b].astype(jnp.float32)
        shape = (8, p.shape[1])
        near, tilt = squares(p)
        a, c = pieces(near), pieces(tilt)
        line = {n: jnp.broadcast_to(p[n : n + 1], shape) for n in range(3)}
        top = rows_of({**line, 3: a[0], 4: a[1], 5: a[2], 6: c[0], 7: c[1]}, shape)
        low = rows_of({0: c[2], 1: 1.0, 2: 1.0, 3: 1.0}, shape)
        feat_ref[b] = jnp.transpose(jnp.concatenate([top, low], 0)).astype(feat_ref.dtype)


def features(reading_pos):
    rb, axes, blk = reading_pos.shape
    return pl.pallas_call(
        reading_features,
        grid=(rb // 16,),
        in_specs=[pl.BlockSpec((16, axes, blk), lambda g: (g, 0, 0))],
        out_specs=pl.BlockSpec((16, blk, ROWS), lambda g: (g, 0, 0)),
        out_shape=jax.ShapeDtypeStruct((rb, blk, ROWS), jnp.bfloat16),
        compiler_params=pltpu.CompilerParams(vmem_limit_bytes=VMEM),
        cost_estimate=pl.CostEstimate(
            flops=0, bytes_accessed=4 * rb * blk * blk, transcendentals=0
        ),
        name="features",
    )(reading_pos)


def make_kernels(cols_ref, pos_ref, all_ref, read_ref, feat_ref, out_ref, weight_ref, fits_ref):
    group, blk, wide = out_ref.shape
    near = wide // blk
    step = pl.program_id(0)
    first = step * group

    @pl.when(step == 0)
    def _():
        far = jnp.maximum(
            jnp.max(jnp.abs(pos_ref[...].astype(jnp.float32))),
            jnp.max(jnp.abs(all_ref[...].astype(jnp.float32))),
        )
        fits_ref[0] = (far <= REACH).astype(jnp.int32)
        shape = (8, blk)

        def prepare(s, carry):
            p = pos_ref[s].astype(jnp.float32)
            x, y, z = (jnp.broadcast_to(p[c : c + 1], shape) for c in range(3))
            close, tilt = squares(p)
            a, c = pieces(close), pieces(tilt)
            left_top = rows_of({0: -2.0 * x, 1: -2.0 * y, 2: -2.0 * z, 3: 1.0, 4: 1.0, 5: 1.0}, shape)
            left_low = rows_of({1: a[0], 2: a[1], 3: a[2]}, shape)
            right_top = rows_of({0: 2.0 * x, 1: 2.0 * y, 2: -4.0 * z, 6: 1.0, 7: 1.0}, shape)
            right_low = rows_of({0: 1.0, 1: c[0], 2: c[1], 3: c[2]}, shape)
            left = jnp.concatenate([left_top, left_low], 0)
            right = jnp.concatenate([right_top, right_low], 0)
            weight_ref[s] = jnp.concatenate([left, right], 1).astype(weight_ref.dtype)
            return carry

        lax.fori_loop(0, pos_ref.shape[0], prepare, 0, unroll=4)

    fits = fits_ref[0] > 0

    @pl.when(fits)
    def _():
        for b in range(group):
            for k in range(0, near, 2):
                both = [
                    jnp.dot(
                        feat_ref[b],
                        weight_ref[cols_ref[first + b, k + c]],
                        preferred_element_type=jnp.float32,
                    )
                    for c in range(2)
                ]
                for r in range(0, blk, 8):
                    pair = []
                    for part in both:
                        inv = lax.rsqrt(part[r : r + 8, :blk])
                        inv2 = inv * inv
                        pair.append((part[r : r + 8, blk:] * (inv2 * inv2)) * inv)
                    out_ref[b, r : r + 8, k * blk : (k + 2) * blk] = jnp.concatenate(
                        pair, 1
                    ).astype(out_ref.dtype)

    @pl.when(jnp.logical_not(fits))
    def _():
        def one_reading(b, carry):
            down = jnp.transpose(read_ref[b].astype(jnp.float32))
            rx, ry, rz = (jnp.broadcast_to(down[:, c : c + 1], (blk, blk)) for c in range(3))

            def one_block(k, carry):
                p = pos_ref[cols_ref[first + b, k]].astype(jnp.float32)
                dx, dy, dz = rx - p[0:1], ry - p[1:2], rz - p[2:3]
                flat, up = dx * dx + dy * dy, dz * dz
                inv = lax.rsqrt(flat + up)
                inv2 = inv * inv
                value = ((up + up - flat) * (inv2 * inv2)) * inv
                out_ref[b, :, pl.ds(pl.multiple_of(k * blk, blk), blk)] = value.astype(
                    out_ref.dtype
                )
                return carry

            return lax.fori_loop(0, near, one_block, carry)

        lax.fori_loop(0, group, one_reading, 0)


def kernel_values(near_cols, slot_p, reading_pos, feat):
    rb, axes, blk = reading_pos.shape
    near = near_cols.shape[1]
    whole = lambda g, *_: (0, 0, 0)
    part = lambda g, *_: (g, 0, 0)
    return pl.pallas_call(
        make_kernels,
        grid_spec=pltpu.PrefetchScalarGridSpec(
            num_scalar_prefetch=1,
            grid=(rb // GEN,),
            in_specs=[
                pl.BlockSpec(slot_p.shape, whole),
                pl.BlockSpec(reading_pos.shape, whole),
                pl.BlockSpec((GEN, axes, blk), part),
                pl.BlockSpec((GEN, blk, ROWS), part),
            ],
            out_specs=pl.BlockSpec((GEN, blk, near * blk), part),
            scratch_shapes=[
                pltpu.VMEM((slot_p.shape[0], ROWS, 2 * blk), jnp.bfloat16),
                pltpu.SMEM((1,), jnp.int32),
            ],
        ),
        out_shape=jax.ShapeDtypeStruct((rb, blk, near * blk), jnp.bfloat16),
        compiler_params=pltpu.CompilerParams(vmem_limit_bytes=VMEM),
        cost_estimate=pl.CostEstimate(
            flops=15 * rb * near * blk * blk,
            bytes_accessed=2 * rb * near * blk * blk,
            transcendentals=rb * near * blk * blk,
        ),
        name="kernel_values",
    )(near_cols, slot_p, reading_pos, reading_pos, feat)


def apply_both(cols_ref, from_ref, to_ref, kern_ref, m_ref, *refs):
    *seen_refs, field_ref, adj_ref, total, obs_ref = refs
    group, blk, wide = kern_ref.shape
    near = wide // blk
    step = pl.program_id(0)

    @pl.when(step == 0)
    def _():
        total[...] = jnp.zeros_like(total)
        share = obs_ref.shape[0] // len(seen_refs)
        for n, ref in enumerate(seen_refs):
            obs_ref[n * share : (n + 1) * share] = ref[...]

    residuals = []
    for b in range(group):
        i = step * group + b
        field = None
        for k in range(0, near, 2):
            part = lax.dot_general(
                jnp.concatenate([m_ref[cols_ref[i, k]], m_ref[cols_ref[i, k + 1]]], 1),
                kern_ref[b, :, k * blk : (k + 2) * blk],
                (((1,), (1,)), ((), ())),
                preferred_element_type=jnp.float32,
            )
            field = part if field is None else field + part
        field = (field * SCALE).astype(jnp.bfloat16)
        field_ref[to_ref[i]] = field
        seen = obs_ref[from_ref[i]].astype(jnp.float32)
        residuals.append((field.astype(jnp.float32) - seen).astype(jnp.bfloat16))
    for b in range(group):
        i = step * group + b
        for k in range(0, near, 2):
            both = jnp.dot(
                residuals[b],
                kern_ref[b, :, k * blk : (k + 2) * blk],
                preferred_element_type=jnp.float32,
            )
            total[cols_ref[i, k]] += both[:, :blk]
            total[cols_ref[i, k + 1]] += both[:, blk:]

    @pl.when(step == pl.num_programs(0) - 1)
    def _():
        adj_ref[...] = (total[...] * SCALE).astype(adj_ref.dtype)


def forward_adjoint(near_cols, from_row, to_row, kern, slot_m, seen):
    rb, blk, wide = kern.shape
    slots, width, _ = slot_m.shape
    whole = lambda g, *_: (0, 0, 0)
    return pl.pallas_call(
        apply_both,
        grid_spec=pltpu.PrefetchScalarGridSpec(
            num_scalar_prefetch=3,
            grid=(rb // USE,),
            in_specs=[
                pl.BlockSpec((USE, blk, wide), lambda g, *_: (g, 0, 0)),
                pl.BlockSpec(slot_m.shape, whole),
                *[pl.BlockSpec(part.shape, whole) for part in seen],
            ],
            out_specs=[pl.BlockSpec((rb, width, blk), whole), pl.BlockSpec((slots, width, blk), whole)],
            scratch_shapes=[
                pltpu.VMEM((slots, width, blk), jnp.float32),
                pltpu.VMEM((rb, width, blk), jnp.bfloat16),
            ],
        ),
        out_shape=[
            jax.ShapeDtypeStruct((rb, width, blk), jnp.bfloat16),
            jax.ShapeDtypeStruct((slots, width, blk), jnp.bfloat16),
        ],
        compiler_params=pltpu.CompilerParams(vmem_limit_bytes=VMEM),
        cost_estimate=pl.CostEstimate(
            flops=4 * width * rb * wide * blk, bytes_accessed=2 * rb * wide * blk, transcendentals=0
        ),
        name="forward_adjoint",
    )(near_cols, from_row, to_row, kern, slot_m, *seen)


def shift(block, axis, by, size):
    return lax.ppermute(block, axis, [(i, (i + by) % size) for i in range(size)])


def add_back(block_ref, live_ref, back_ref, out_ref):
    out_ref[...] = jnp.zeros_like(out_ref)

    def one(s, carry):
        alive = live_ref[s] > 0
        out_ref[block_ref[s]] += jnp.where(alive, back_ref[s].astype(jnp.float32), 0.0)
        return carry

    lax.fori_loop(0, back_ref.shape[0], one, 0, unroll=4)


def combine(flat_index, live, back, old):
    _, width, depth = back.shape
    return pl.pallas_call(
        add_back,
        grid_spec=pltpu.PrefetchScalarGridSpec(
            num_scalar_prefetch=2,
            grid=(1,),
            in_specs=[pl.BlockSpec(back.shape, lambda g, *_: (0, 0, 0))],
            out_specs=pl.BlockSpec((old, width, depth), lambda g, *_: (0, 0, 0)),
        ),
        out_shape=jax.ShapeDtypeStruct((old, width, depth), jnp.float32),
        compiler_params=pltpu.CompilerParams(vmem_limit_bytes=VMEM),
        name="combine",
    )(flat_index, live, back)


def on_device(
    moments, dipole_pos, send_index, send_count, reading_pos, near_cols, grid_slot, observed
):
    peers = lax.axis_size("morton")
    tiles = lax.axis_size("tile")
    cap = send_index.shape[1]
    old, width, depth = moments.shape
    rb = reading_pos.shape[0]
    share = rb // tiles
    swap = functools.partial(lax.all_to_all, split_axis=0, concat_axis=0, tiled=True)
    live = (jnp.arange(cap)[None, :] < send_count[:, None]).reshape(-1)
    flat_index = send_index.reshape(-1)
    send_p = dipole_pos[flat_index]
    slot_p = swap(send_p.reshape(peers, cap, 3, depth), "morton").reshape(peers * cap, 3, depth)
    me = lax.axis_index("tile")
    to_tile, within = grid_slot // rb, grid_slot % share
    from_row = (me - to_tile) % tiles * share + within
    to_row = (to_tile - me) % tiles * share + within
    seen = []
    for by in range(tiles):
        part = lax.dynamic_slice_in_dim(observed, (me + by) % tiles * share, share, 0)
        seen.append(shift(part, "tile", by, tiles) if by else part)
    feat = features(reading_pos)
    send_m = jnp.where(live[:, None, None], moments[flat_index], jnp.zeros((), jnp.bfloat16))
    send_m, feat, seen[1], seen[2] = lax.optimization_barrier((send_m, feat, seen[1], seen[2]))
    slot_m = swap(send_m.reshape(peers, cap, width, depth), "morton").reshape(
        peers * cap, width, depth
    )
    kern = kernel_values(near_cols, slot_p, reading_pos, feat)
    ordered, slot_adj = forward_adjoint(near_cols, from_row, to_row, kern, slot_m, seen)
    back = swap(slot_adj.reshape(peers, cap, width, depth), "morton").reshape(
        peers * cap, width, depth
    )
    field = jnp.zeros_like(ordered)
    for by in range(tiles):
        part = ordered[by * share : (by + 1) * share]
        part = shift(part, "tile", by, tiles) if by else part
        field = lax.dynamic_update_slice_in_dim(field, part, (me - by) % tiles * share, 0)
    adjoint_moments = combine(flat_index, live.astype(jnp.int32), back, old)
    return (field, adjoint_moments)


def solution(mesh):
    return jax.shard_map(
        on_device,
        mesh=mesh,
        in_specs=(
            P(("morton", "tile"), None, None),
            P(("morton", "tile"), None, None),
            P(("morton", "tile"), None),
            P(("morton", "tile")),
            P(("morton", "tile"), None, None),
            P(("morton", "tile"), None),
            P(("morton", "tile")),
            P(("morton", "tile"), None, None),
        ),
        out_specs=(P(("morton", "tile"), None, None), P(("morton", "tile"), None, None)),
        check_vma=False,
    )
```

```python
import functools

import jax
import jax.numpy as jnp
from jax import lax
from jax.experimental import pallas as pl
from jax.experimental.pallas import tpu as pltpu
from jax.sharding import PartitionSpec as P

SCALE = 0.2
REACH = 64.0
GEN = 8
USE = 8
ROWS = 16
VMEM = 50 * 2**20


def pick_places(index_ref, pos_ref, out_ref, pos32):
    axes, _, blk = pos_ref.shape
    pos32[...] = pos_ref[...].astype(jnp.float32)
    for q in range(out_ref.shape[0]):
        lines = {}
        for c in range(index_ref.shape[0]):
            for n in range(axes):
                line = pos32[n, pl.ds(index_ref[c, q], 1), :]
                lines[c * axes + n] = jnp.broadcast_to(line, (8, blk))
        out_ref[q] = rows_of(lines, (8, blk)).astype(out_ref.dtype)


def pick_moments(index_ref, count_ref, m_ref, out_ref):
    def one(q, carry):
        for c in range(index_ref.shape[0]):
            kept = jnp.where(count_ref[q] > c, m_ref[index_ref[c, q]].astype(jnp.float32), 0.0)
            out_ref[q, c] = kept.astype(out_ref.dtype)
        return carry

    lax.fori_loop(0, index_ref.shape[1], one, 0, unroll=8)


def picked(kernel, scalars, table, out_shape, scratch, name):
    return pl.pallas_call(
        kernel,
        grid_spec=pltpu.PrefetchScalarGridSpec(
            num_scalar_prefetch=len(scalars),
            grid=(1,),
            in_specs=[pl.BlockSpec(table.shape, lambda g, *_: (0,) * table.ndim)],
            out_specs=pl.BlockSpec(out_shape, lambda g, *_: (0,) * len(out_shape)),
            scratch_shapes=scratch,
        ),
        out_shape=jax.ShapeDtypeStruct(out_shape, table.dtype),
        compiler_params=pltpu.CompilerParams(vmem_limit_bytes=60 * 2**20),
        cost_estimate=pl.CostEstimate(flops=0, bytes_accessed=1024, transcendentals=0),
        name=name,
    )(*scalars, table)


def squares(x, y, z):
    x, y, z = x * x, y * y, z * z
    return x + y + z, 2.0 * z - x - y


def pieces(value):
    high = value.astype(jnp.bfloat16).astype(jnp.float32)
    rest = value - high
    middle = rest.astype(jnp.bfloat16).astype(jnp.float32)
    return high, middle, rest - middle


def rows_of(table, shape):
    row = lax.broadcasted_iota(jnp.int32, shape, 0)
    out = jnp.zeros(shape, jnp.float32)
    for at, value in table.items():
        out = jnp.where(row == at, value, out)
    return out


def reading_features(read_ref, feat_ref, far_ref):
    x, y, z = (read_ref[c].astype(jnp.float32) for c in range(3))
    close, tilt = squares(x, y, z)
    lines = [x, y, z, *pieces(close), *pieces(tilt)]
    shape = (8, x.shape[1])
    size = jnp.maximum(jnp.maximum(jnp.abs(x), jnp.abs(y)), jnp.abs(z))
    far = functools.reduce(jnp.maximum, [size[r : r + 8] for r in range(0, size.shape[0], 8)])
    first = pl.program_id(0) == 0
    far_ref[...] = jnp.maximum(jnp.where(first, 0.0, far_ref[...]), far)
    for b in range(feat_ref.shape[0]):
        line = [jnp.broadcast_to(v[b : b + 1], shape) for v in lines]
        top = rows_of(dict(enumerate(line[:8])), shape)
        low = rows_of({0: line[8], 1: 1.0, 2: 1.0, 3: 1.0}, shape)
        feat_ref[b] = jnp.transpose(jnp.concatenate([top, low], 0)).astype(feat_ref.dtype)


def features(reading_pos):
    axes, rb, blk = reading_pos.shape
    return pl.pallas_call(
        reading_features,
        grid=(rb // 16,),
        in_specs=[pl.BlockSpec((axes, 16, blk), lambda g: (0, g, 0))],
        out_specs=[
            pl.BlockSpec((16, blk, ROWS), lambda g: (g, 0, 0)),
            pl.BlockSpec((8, blk), lambda g: (0, 0)),
        ],
        out_shape=[
            jax.ShapeDtypeStruct((rb, blk, ROWS), jnp.bfloat16),
            jax.ShapeDtypeStruct((8, blk), jnp.float32),
        ],
        compiler_params=pltpu.CompilerParams(vmem_limit_bytes=VMEM),
        cost_estimate=pl.CostEstimate(
            flops=0, bytes_accessed=4 * rb * blk * blk, transcendentals=0
        ),
        name="features",
    )(reading_pos)


def make_kernels(cols_ref, pos_ref, far_ref, feat_ref, out_ref, weight_ref, fits_ref):
    group, blk, wide = out_ref.shape
    near = wide // blk
    axes = 3
    step = pl.program_id(0)
    first = step * group

    @pl.when(step == 0)
    def _():
        far = jnp.maximum(
            jnp.max(jnp.abs(pos_ref[...].astype(jnp.float32))), jnp.max(far_ref[...])
        )
        fits_ref[0] = (far <= REACH).astype(jnp.int32)
        shape = (8, blk)

        def prepare(q, carry):
            p = pos_ref[q].astype(jnp.float32)
            for c in range(2):
                x, y, z = (
                    jnp.broadcast_to(p[c * axes + n : c * axes + n + 1], shape) for n in range(axes)
                )
                close, tilt = squares(x, y, z)
                a, t = pieces(close), pieces(tilt)
                lines = (
                    {0: -2.0 * x, 1: -2.0 * y, 2: -2.0 * z, 3: 1.0, 4: 1.0, 5: 1.0},
                    {1: a[0], 2: a[1], 3: a[2]},
                    {0: 2.0 * x, 1: 2.0 * y, 2: -4.0 * z, 6: 1.0, 7: 1.0},
                    {0: 1.0, 1: t[0], 2: t[1], 3: t[2]},
                )
                part = [rows_of(line, shape) for line in lines]
                left = jnp.concatenate(part[:2], 0)
                right = jnp.concatenate(part[2:], 0)
                both = jnp.concatenate([left, right], 1)
                weight_ref[2 * q + c] = both.astype(weight_ref.dtype)
            return carry

        lax.fori_loop(0, pos_ref.shape[0], prepare, 0, unroll=2)

    fits = fits_ref[0] > 0

    @pl.when(fits)
    def _():
        for b in range(group):
            for k in range(0, near, 2):
                both = [
                    jnp.dot(
                        feat_ref[b],
                        weight_ref[cols_ref[k + c, first + b]],
                        preferred_element_type=jnp.float32,
                    )
                    for c in range(2)
                ]
                for r in range(0, blk, 8):
                    pair = []
                    for part in both:
                        inv = lax.rsqrt(part[r : r + 8, :blk])
                        inv2 = inv * inv
                        pair.append((SCALE * part[r : r + 8, blk:]) * (inv2 * inv2) * inv)
                    out_ref[b, r : r + 8, k * blk : (k + 2) * blk] = jnp.concatenate(
                        pair, 1
                    ).astype(out_ref.dtype)

    @pl.when(jnp.logical_not(fits))
    def _():
        def one_reading(b, carry):
            place = feat_ref[b].astype(jnp.float32)
            rx, ry, rz = (
                jnp.broadcast_to(place[:, c : c + 1], (blk, blk)) for c in range(axes)
            )

            def one_block(k, carry):
                s = cols_ref[k, first + b]
                p = pos_ref[lax.div(s, 2)].astype(jnp.float32)
                odd = lax.rem(s, 2) > 0
                px, py, pz = (
                    jnp.where(odd, p[axes + c : axes + c + 1], p[c : c + 1]) for c in range(axes)
                )
                dx, dy, dz = rx - px, ry - py, rz - pz
                flat, up = dx * dx + dy * dy, dz * dz
                inv = lax.rsqrt(flat + up)
                inv2 = inv * inv
                value = (SCALE * (up + up - flat)) * (inv2 * inv2) * inv
                out_ref[b, :, pl.ds(pl.multiple_of(k * blk, blk), blk)] = value.astype(
                    out_ref.dtype
                )
                return carry

            return lax.fori_loop(0, near, one_block, carry)

        lax.fori_loop(0, group, one_reading, 0)


def kernel_values(near_cols, slot_p, far, feat):
    rb, blk, _ = feat.shape
    near = near_cols.shape[0]
    whole = lambda g, *_: (0, 0, 0)
    part = lambda g, *_: (g, 0, 0)
    return pl.pallas_call(
        make_kernels,
        grid_spec=pltpu.PrefetchScalarGridSpec(
            num_scalar_prefetch=1,
            grid=(rb // GEN,),
            in_specs=[
                pl.BlockSpec(slot_p.shape, whole),
                pl.BlockSpec(far.shape, lambda g, *_: (0, 0)),
                pl.BlockSpec((GEN, blk, ROWS), part),
            ],
            out_specs=pl.BlockSpec((GEN, blk, near * blk), part),
            scratch_shapes=[
                pltpu.VMEM((2 * slot_p.shape[0], ROWS, 2 * blk), jnp.bfloat16),
                pltpu.SMEM((1,), jnp.int32),
            ],
        ),
        out_shape=jax.ShapeDtypeStruct((rb, blk, near * blk), jnp.bfloat16),
        compiler_params=pltpu.CompilerParams(vmem_limit_bytes=VMEM),
        cost_estimate=pl.CostEstimate(
            flops=15 * rb * near * blk * blk,
            bytes_accessed=2 * rb * near * blk * blk,
            transcendentals=rb * near * blk * blk,
        ),
        name="kernel_values",
    )(near_cols, slot_p, far, feat)


def apply_both(cols_ref, slot_ref, me_ref, kern_ref, m_ref, *refs):
    *seen_refs, field_ref, adj_ref, total, obs_ref = refs
    group, blk, wide = kern_ref.shape
    near = wide // blk
    step = pl.program_id(0)
    tiles, rb, me = len(seen_refs), obs_ref.shape[0], me_ref[0]
    share = rb // tiles

    @pl.when(step == 0)
    def _():
        total[...] = jnp.zeros_like(total)
        for n, ref in enumerate(seen_refs):
            obs_ref[n * share : (n + 1) * share] = ref[...]

    residuals = []
    for b in range(group):
        i = step * group + b
        field = None
        for k in range(0, near, 2):
            part = lax.dot_general(
                jnp.concatenate([m_ref[cols_ref[k, i]], m_ref[cols_ref[k + 1, i]]], 1),
                kern_ref[b, :, k * blk : (k + 2) * blk],
                (((1,), (1,)), ((), ())),
                preferred_element_type=jnp.float32,
            )
            field = part if field is None else field + part
        field = field.astype(jnp.bfloat16)
        there = lax.div(slot_ref[i], rb)
        within = lax.rem(slot_ref[i], share)
        field_ref[lax.rem(there + tiles - me, tiles) * share + within] = field
        row = lax.rem(me + tiles - there, tiles) * share + within
        seen = obs_ref[row].astype(jnp.float32)
        residuals.append((field.astype(jnp.float32) - seen).astype(jnp.bfloat16))
    for b in range(group):
        i = step * group + b
        for k in range(0, near, 2):
            both = jnp.dot(
                residuals[b],
                kern_ref[b, :, k * blk : (k + 2) * blk],
                preferred_element_type=jnp.float32,
            )
            total[cols_ref[k, i]] += both[:, :blk]
            total[cols_ref[k + 1, i]] += both[:, blk:]

    @pl.when(step == pl.num_programs(0) - 1)
    def _():
        adj_ref[...] = total[...].astype(adj_ref.dtype)


def forward_adjoint(near_cols, grid_slot, me, kern, slot_m, seen):
    rb, blk, wide = kern.shape
    slots, width, _ = slot_m.shape
    whole = lambda g, *_: (0, 0, 0)
    return pl.pallas_call(
        apply_both,
        grid_spec=pltpu.PrefetchScalarGridSpec(
            num_scalar_prefetch=3,
            grid=(rb // USE,),
            in_specs=[
                pl.BlockSpec((USE, blk, wide), lambda g, *_: (g, 0, 0)),
                pl.BlockSpec(slot_m.shape, whole),
                *[pl.BlockSpec(part.shape, whole) for part in seen],
            ],
            out_specs=[pl.BlockSpec((rb, width, blk), whole), pl.BlockSpec((slots, width, blk), whole)],
            scratch_shapes=[
                pltpu.VMEM((slots, width, blk), jnp.float32),
                pltpu.VMEM((rb, width, blk), jnp.bfloat16),
            ],
        ),
        out_shape=[
            jax.ShapeDtypeStruct((rb, width, blk), jnp.bfloat16),
            jax.ShapeDtypeStruct((slots, width, blk), jnp.bfloat16),
        ],
        compiler_params=pltpu.CompilerParams(vmem_limit_bytes=VMEM),
        cost_estimate=pl.CostEstimate(
            flops=4 * width * rb * wide * blk, bytes_accessed=2 * rb * wide * blk, transcendentals=0
        ),
        name="forward_adjoint",
    )(near_cols, grid_slot, me, kern, slot_m, *seen)


def shift(block, axis, by, size):
    return lax.ppermute(block, axis, [(i, (i + by) % size) for i in range(size)])


def add_back(index_ref, count_ref, back_ref, out_ref):
    out_ref[...] = jnp.zeros_like(out_ref)

    def one(q, carry):
        for c in range(back_ref.shape[1]):
            value = back_ref[q, c].astype(jnp.float32)
            out_ref[index_ref[c, q]] += jnp.where(count_ref[q] > c, value, 0.0)
        return carry

    lax.fori_loop(0, back_ref.shape[0], one, 0, unroll=2)


def combine(send_index, send_count, back, old):
    _, _, width, depth = back.shape
    return pl.pallas_call(
        add_back,
        grid_spec=pltpu.PrefetchScalarGridSpec(
            num_scalar_prefetch=2,
            grid=(1,),
            in_specs=[pl.BlockSpec(back.shape, lambda g, *_: (0, 0, 0, 0))],
            out_specs=pl.BlockSpec((old, width, depth), lambda g, *_: (0, 0, 0)),
        ),
        out_shape=jax.ShapeDtypeStruct((old, width, depth), jnp.float32),
        compiler_params=pltpu.CompilerParams(vmem_limit_bytes=VMEM),
        name="combine",
    )(send_index, send_count, back)


def on_device(
    moments, dipole_pos, send_index, send_count, reading_pos, near_cols, grid_slot, observed
):
    peers = lax.axis_size("morton")
    tiles = lax.axis_size("tile")
    cap = send_index.shape[1]
    old, width, depth = moments.shape
    rb = reading_pos.shape[0]
    share = rb // tiles
    swap = functools.partial(lax.all_to_all, split_axis=0, concat_axis=0, tiled=True)
    send_index, near_cols = send_index.T, near_cols.T
    dipole_pos, reading_pos = (jnp.swapaxes(a, 0, 1) for a in (dipole_pos, reading_pos))
    send_p = picked(
        pick_places,
        (send_index,),
        dipole_pos,
        (peers, 8, depth),
        [pltpu.VMEM(dipole_pos.shape, jnp.float32)],
        "pick_places",
    )
    send_m = picked(
        pick_moments,
        (send_index, send_count),
        moments,
        (peers, cap, width, depth),
        [],
        "pick_moments",
    )
    slot_p = swap(send_p, "morton")
    feat, far = features(reading_pos)
    feat, observed = lax.optimization_barrier((feat, observed))
    me = lax.axis_index("tile")
    seen = [
        lax.dynamic_slice_in_dim(observed, (me + by) % tiles * share, share, 0)
        for by in range(tiles)
    ]
    slot_p, *seen = lax.optimization_barrier((slot_p, *seen))
    send_m, feat, *seen = lax.optimization_barrier((send_m, feat, *seen))
    seen = [shift(part, "tile", by, tiles) if by else part for by, part in enumerate(seen)]
    slot_m = swap(send_m, "morton").reshape(peers * cap, width, depth)
    kern = kernel_values(near_cols, slot_p, far, feat)
    ordered, slot_adj = forward_adjoint(near_cols, grid_slot, me.reshape(1), kern, slot_m, seen)
    back = swap(slot_adj.reshape(peers, cap, width, depth), "morton")
    field = jnp.zeros_like(ordered)
    for by in range(tiles):
        part = ordered[by * share : (by + 1) * share]
        part = shift(part, "tile", by, tiles) if by else part
        field = lax.dynamic_update_slice_in_dim(field, part, (me - by) % tiles * share, 0)
    adjoint_moments = combine(send_index, send_count, back, old)
    return (field, adjoint_moments)


def solution(mesh):
    return jax.shard_map(
        on_device,
        mesh=mesh,
        in_specs=(
            P(("morton", "tile"), None, None),
            P(("morton", "tile"), None, None),
            P(("morton", "tile"), None),
            P(("morton", "tile")),
            P(("morton", "tile"), None, None),
            P(("morton", "tile"), None),
            P(("morton", "tile")),
            P(("morton", "tile"), None, None),
        ),
        out_specs=(P(("morton", "tile"), None, None), P(("morton", "tile"), None, None)),
        check_vma=False,
    )
```

```python
import functools

import jax
import jax.numpy as jnp
from jax import lax
from jax.experimental import pallas as pl
from jax.experimental.pallas import tpu as pltpu
from jax.sharding import PartitionSpec as P

SCALE = 0.2
REACH = 64.0
GEN = 8
USE = 8
LAG = 3
ROWS = 16
VMEM = 50 * 2**20


def pick_places(index_ref, pos_ref, out_ref, pos32):
    axes, _, blk = pos_ref.shape
    pos32[...] = pos_ref[...].astype(jnp.float32)
    for q in range(out_ref.shape[0]):
        lines = {}
        for c in range(index_ref.shape[0]):
            for n in range(axes):
                line = pos32[n, pl.ds(index_ref[c, q], 1), :]
                lines[c * axes + n] = jnp.broadcast_to(line, (8, blk))
        out_ref[q] = rows_of(lines, (8, blk)).astype(out_ref.dtype)


def pick_moments(index_ref, count_ref, m_ref, out_ref):
    def one(q, carry):
        for c in range(index_ref.shape[0]):
            kept = jnp.where(count_ref[q] > c, m_ref[index_ref[c, q]].astype(jnp.float32), 0.0)
            out_ref[q, c] = kept.astype(out_ref.dtype)
        return carry

    lax.fori_loop(0, index_ref.shape[1], one, 0, unroll=8)


def picked(kernel, scalars, table, out_shape, scratch, name):
    return pl.pallas_call(
        kernel,
        grid_spec=pltpu.PrefetchScalarGridSpec(
            num_scalar_prefetch=len(scalars),
            grid=(1,),
            in_specs=[pl.BlockSpec(table.shape, lambda g, *_: (0,) * table.ndim)],
            out_specs=pl.BlockSpec(out_shape, lambda g, *_: (0,) * len(out_shape)),
            scratch_shapes=scratch,
        ),
        out_shape=jax.ShapeDtypeStruct(out_shape, table.dtype),
        compiler_params=pltpu.CompilerParams(vmem_limit_bytes=60 * 2**20),
        cost_estimate=pl.CostEstimate(flops=0, bytes_accessed=1024, transcendentals=0),
        name=name,
    )(*scalars, table)


def squares(x, y, z):
    x, y, z = x * x, y * y, z * z
    return x + y + z, 2.0 * z - x - y


def pieces(value):
    high = value.astype(jnp.bfloat16).astype(jnp.float32)
    rest = value - high
    middle = rest.astype(jnp.bfloat16).astype(jnp.float32)
    return high, middle, rest - middle


def rows_of(table, shape):
    row = lax.broadcasted_iota(jnp.int32, shape, 0)
    out = jnp.zeros(shape, jnp.float32)
    for at, value in table.items():
        out = jnp.where(row == at, value, out)
    return out


def reading_features(read_ref, feat_ref, far_ref):
    x, y, z = (read_ref[c].astype(jnp.float32) for c in range(3))
    close, tilt = squares(x, y, z)
    lines = [x, y, z, *pieces(close), *pieces(tilt)]
    shape = (8, x.shape[1])
    size = jnp.maximum(jnp.maximum(jnp.abs(x), jnp.abs(y)), jnp.abs(z))
    far = functools.reduce(jnp.maximum, [size[r : r + 8] for r in range(0, size.shape[0], 8)])
    first = pl.program_id(0) == 0
    far_ref[...] = jnp.maximum(jnp.where(first, 0.0, far_ref[...]), far)
    for b in range(feat_ref.shape[0]):
        line = [jnp.broadcast_to(v[b : b + 1], shape) for v in lines]
        top = rows_of(dict(enumerate(line[:8])), shape)
        low = rows_of({0: line[8], 1: 1.0, 2: 1.0, 3: 1.0}, shape)
        feat_ref[b] = jnp.transpose(jnp.concatenate([top, low], 0)).astype(feat_ref.dtype)


def features(reading_pos):
    axes, rb, blk = reading_pos.shape
    return pl.pallas_call(
        reading_features,
        grid=(rb // 16,),
        in_specs=[pl.BlockSpec((axes, 16, blk), lambda g: (0, g, 0))],
        out_specs=[
            pl.BlockSpec((16, blk, ROWS), lambda g: (g, 0, 0)),
            pl.BlockSpec((8, blk), lambda g: (0, 0)),
        ],
        out_shape=[
            jax.ShapeDtypeStruct((rb, blk, ROWS), jnp.bfloat16),
            jax.ShapeDtypeStruct((8, blk), jnp.float32),
        ],
        compiler_params=pltpu.CompilerParams(vmem_limit_bytes=VMEM),
        cost_estimate=pl.CostEstimate(
            flops=0, bytes_accessed=4 * rb * blk * blk, transcendentals=0
        ),
        name="features",
    )(reading_pos)


def make_kernels(cols_ref, pos_ref, far_ref, feat_ref, out_ref, weight_ref, fits_ref):
    group, blk, wide = out_ref.shape
    near = wide // blk
    axes = 3
    step = pl.program_id(0)
    first = step * group

    @pl.when(step == 0)
    def _():
        far = jnp.maximum(
            jnp.max(jnp.abs(pos_ref[...].astype(jnp.float32))), jnp.max(far_ref[...])
        )
        fits_ref[0] = (far <= REACH).astype(jnp.int32)
        shape = (8, blk)

        def prepare(q, carry):
            p = pos_ref[q].astype(jnp.float32)
            for c in range(2):
                x, y, z = (
                    jnp.broadcast_to(p[c * axes + n : c * axes + n + 1], shape) for n in range(axes)
                )
                close, tilt = squares(x, y, z)
                a, t = pieces(close), pieces(tilt)
                lines = (
                    {0: -2.0 * x, 1: -2.0 * y, 2: -2.0 * z, 3: 1.0, 4: 1.0, 5: 1.0},
                    {1: a[0], 2: a[1], 3: a[2]},
                    {0: 2.0 * x, 1: 2.0 * y, 2: -4.0 * z, 6: 1.0, 7: 1.0},
                    {0: 1.0, 1: t[0], 2: t[1], 3: t[2]},
                )
                part = [rows_of(line, shape) for line in lines]
                left = jnp.concatenate(part[:2], 0)
                right = jnp.concatenate(part[2:], 0)
                both = jnp.concatenate([left, right], 1)
                weight_ref[2 * q + c] = both.astype(weight_ref.dtype)
            return carry

        lax.fori_loop(0, pos_ref.shape[0], prepare, 0, unroll=2)

    fits = fits_ref[0] > 0

    @pl.when(fits)
    def _():
        for b in range(group):
            for k in range(0, near, 2):
                both = [
                    jnp.dot(
                        feat_ref[b],
                        weight_ref[cols_ref[k + c, first + b]],
                        preferred_element_type=jnp.float32,
                    )
                    for c in range(2)
                ]
                for r in range(0, blk, 8):
                    pair = []
                    for part in both:
                        inv = lax.rsqrt(part[r : r + 8, :blk])
                        inv2 = inv * inv
                        pair.append((SCALE * part[r : r + 8, blk:]) * (inv2 * inv2) * inv)
                    out_ref[b, r : r + 8, k * blk : (k + 2) * blk] = jnp.concatenate(
                        pair, 1
                    ).astype(out_ref.dtype)

    @pl.when(jnp.logical_not(fits))
    def _():
        def one_reading(b, carry):
            place = feat_ref[b].astype(jnp.float32)
            rx, ry, rz = (
                jnp.broadcast_to(place[:, c : c + 1], (blk, blk)) for c in range(axes)
            )

            def one_block(k, carry):
                s = cols_ref[k, first + b]
                p = pos_ref[lax.div(s, 2)].astype(jnp.float32)
                odd = lax.rem(s, 2) > 0
                px, py, pz = (
                    jnp.where(odd, p[axes + c : axes + c + 1], p[c : c + 1]) for c in range(axes)
                )
                dx, dy, dz = rx - px, ry - py, rz - pz
                flat, up = dx * dx + dy * dy, dz * dz
                inv = lax.rsqrt(flat + up)
                inv2 = inv * inv
                value = (SCALE * (up + up - flat)) * (inv2 * inv2) * inv
                out_ref[b, :, pl.ds(pl.multiple_of(k * blk, blk), blk)] = value.astype(
                    out_ref.dtype
                )
                return carry

            return lax.fori_loop(0, near, one_block, carry)

        lax.fori_loop(0, group, one_reading, 0)


def kernel_values(near_cols, slot_p, far, feat):
    rb, blk, _ = feat.shape
    near = near_cols.shape[0]
    whole = lambda g, *_: (0, 0, 0)
    part = lambda g, *_: (g, 0, 0)
    return pl.pallas_call(
        make_kernels,
        grid_spec=pltpu.PrefetchScalarGridSpec(
            num_scalar_prefetch=1,
            grid=(rb // GEN,),
            in_specs=[
                pl.BlockSpec(slot_p.shape, whole),
                pl.BlockSpec(far.shape, lambda g, *_: (0, 0)),
                pl.BlockSpec((GEN, blk, ROWS), part),
            ],
            out_specs=pl.BlockSpec((GEN, blk, near * blk), part),
            scratch_shapes=[
                pltpu.VMEM((2 * slot_p.shape[0], ROWS, 2 * blk), jnp.bfloat16),
                pltpu.SMEM((1,), jnp.int32),
            ],
        ),
        out_shape=jax.ShapeDtypeStruct((rb, blk, near * blk), jnp.bfloat16),
        compiler_params=pltpu.CompilerParams(vmem_limit_bytes=VMEM),
        cost_estimate=pl.CostEstimate(
            flops=15 * rb * near * blk * blk,
            bytes_accessed=2 * rb * near * blk * blk,
            transcendentals=rb * near * blk * blk,
        ),
        name="kernel_values",
    )(near_cols, slot_p, far, feat)


def apply_both(cols_ref, slot_ref, me_ref, kern_ref, m_ref, *refs):
    *seen_refs, field_ref, adj_ref, total, obs_ref = refs
    group, blk, wide = kern_ref.shape
    near = wide // blk
    step = pl.program_id(0)
    tiles, rb, me = len(seen_refs), obs_ref.shape[0], me_ref[0]
    share = rb // tiles

    @pl.when(step == 0)
    def _():
        total[...] = jnp.zeros_like(total)
        for n, ref in enumerate(seen_refs):
            obs_ref[n * share : (n + 1) * share] = ref[...]

    def forward(b):
        i = step * group + b
        field = None
        for k in range(0, near, 2):
            part = lax.dot_general(
                jnp.concatenate([m_ref[cols_ref[k, i]], m_ref[cols_ref[k + 1, i]]], 1),
                kern_ref[b, :, k * blk : (k + 2) * blk],
                (((1,), (1,)), ((), ())),
                preferred_element_type=jnp.float32,
            )
            field = part if field is None else field + part
        field = field.astype(jnp.bfloat16)
        there = lax.div(slot_ref[i], rb)
        within = lax.rem(slot_ref[i], share)
        field_ref[lax.rem(there + tiles - me, tiles) * share + within] = field
        row = lax.rem(me + tiles - there, tiles) * share + within
        seen = obs_ref[row].astype(jnp.float32)
        return (field.astype(jnp.float32) - seen).astype(jnp.bfloat16)

    def adjoint(b, residual):
        i = step * group + b
        for k in range(0, near, 2):
            both = jnp.dot(
                residual,
                kern_ref[b, :, k * blk : (k + 2) * blk],
                preferred_element_type=jnp.float32,
            )
            total[cols_ref[k, i]] += both[:, :blk]
            total[cols_ref[k + 1, i]] += both[:, blk:]

    residuals = []
    for b in range(group):
        residuals.append(forward(b))
        if b >= LAG:
            adjoint(b - LAG, residuals[b - LAG])
    for b in range(group - LAG, group):
        adjoint(b, residuals[b])

    @pl.when(step == pl.num_programs(0) - 1)
    def _():
        adj_ref[...] = total[...].astype(adj_ref.dtype)


def forward_adjoint(near_cols, grid_slot, me, kern, slot_m, seen):
    rb, blk, wide = kern.shape
    slots, width, _ = slot_m.shape
    whole = lambda g, *_: (0, 0, 0)
    return pl.pallas_call(
        apply_both,
        grid_spec=pltpu.PrefetchScalarGridSpec(
            num_scalar_prefetch=3,
            grid=(rb // USE,),
            in_specs=[
                pl.BlockSpec((USE, blk, wide), lambda g, *_: (g, 0, 0)),
                pl.BlockSpec(slot_m.shape, whole),
                *[pl.BlockSpec(part.shape, whole) for part in seen],
            ],
            out_specs=[pl.BlockSpec((rb, width, blk), whole), pl.BlockSpec((slots, width, blk), whole)],
            scratch_shapes=[
                pltpu.VMEM((slots, width, blk), jnp.float32),
                pltpu.VMEM((rb, width, blk), jnp.bfloat16),
            ],
        ),
        out_shape=[
            jax.ShapeDtypeStruct((rb, width, blk), jnp.bfloat16),
            jax.ShapeDtypeStruct((slots, width, blk), jnp.bfloat16),
        ],
        compiler_params=pltpu.CompilerParams(vmem_limit_bytes=VMEM),
        cost_estimate=pl.CostEstimate(
            flops=4 * width * rb * wide * blk, bytes_accessed=2 * rb * wide * blk, transcendentals=0
        ),
        name="forward_adjoint",
    )(near_cols, grid_slot, me, kern, slot_m, *seen)


def shift(block, axis, by, size):
    return lax.ppermute(block, axis, [(i, (i + by) % size) for i in range(size)])


def add_back(index_ref, count_ref, back_ref, out_ref):
    out_ref[...] = jnp.zeros_like(out_ref)

    def one(q, carry):
        for c in range(back_ref.shape[1]):
            value = back_ref[q, c].astype(jnp.float32)
            out_ref[index_ref[c, q]] += jnp.where(count_ref[q] > c, value, 0.0)
        return carry

    lax.fori_loop(0, back_ref.shape[0], one, 0, unroll=2)


def combine(send_index, send_count, back, old):
    _, _, width, depth = back.shape
    return pl.pallas_call(
        add_back,
        grid_spec=pltpu.PrefetchScalarGridSpec(
            num_scalar_prefetch=2,
            grid=(1,),
            in_specs=[pl.BlockSpec(back.shape, lambda g, *_: (0, 0, 0, 0))],
            out_specs=pl.BlockSpec((old, width, depth), lambda g, *_: (0, 0, 0)),
        ),
        out_shape=jax.ShapeDtypeStruct((old, width, depth), jnp.float32),
        compiler_params=pltpu.CompilerParams(vmem_limit_bytes=VMEM),
        name="combine",
    )(send_index, send_count, back)


def on_device(
    moments, dipole_pos, send_index, send_count, reading_pos, near_cols, grid_slot, observed
):
    peers = lax.axis_size("morton")
    tiles = lax.axis_size("tile")
    cap = send_index.shape[1]
    old, width, depth = moments.shape
    rb = reading_pos.shape[0]
    share = rb // tiles
    swap = functools.partial(lax.all_to_all, split_axis=0, concat_axis=0, tiled=True)
    send_index, near_cols = send_index.T, near_cols.T
    dipole_pos, reading_pos = (jnp.swapaxes(a, 0, 1) for a in (dipole_pos, reading_pos))
    send_p = picked(
        pick_places,
        (send_index,),
        dipole_pos,
        (peers, 8, depth),
        [pltpu.VMEM(dipole_pos.shape, jnp.float32)],
        "pick_places",
    )
    send_m = picked(
        pick_moments,
        (send_index, send_count),
        moments,
        (peers, cap, width, depth),
        [],
        "pick_moments",
    )
    slot_p = swap(send_p, "morton")
    feat, far = features(reading_pos)
    feat, observed = lax.optimization_barrier((feat, observed))
    me = lax.axis_index("tile")
    seen = [
        lax.dynamic_slice_in_dim(observed, (me + by) % tiles * share, share, 0)
        for by in range(tiles)
    ]
    slot_p, *seen = lax.optimization_barrier((slot_p, *seen))
    send_m, feat, *seen = lax.optimization_barrier((send_m, feat, *seen))
    seen = [shift(part, "tile", by, tiles) if by else part for by, part in enumerate(seen)]
    slot_m = swap(send_m, "morton").reshape(peers * cap, width, depth)
    kern = kernel_values(near_cols, slot_p, far, feat)
    ordered, slot_adj = forward_adjoint(near_cols, grid_slot, me.reshape(1), kern, slot_m, seen)
    back = swap(slot_adj.reshape(peers, cap, width, depth), "morton")
    field = jnp.zeros_like(ordered)
    for by in range(tiles):
        part = ordered[by * share : (by + 1) * share]
        part = shift(part, "tile", by, tiles) if by else part
        field = lax.dynamic_update_slice_in_dim(field, part, (me - by) % tiles * share, 0)
    adjoint_moments = combine(send_index, send_count, back, old)
    return (field, adjoint_moments)


def solution(mesh):
    return jax.shard_map(
        on_device,
        mesh=mesh,
        in_specs=(
            P(("morton", "tile"), None, None),
            P(("morton", "tile"), None, None),
            P(("morton", "tile"), None),
            P(("morton", "tile")),
            P(("morton", "tile"), None, None),
            P(("morton", "tile"), None),
            P(("morton", "tile")),
            P(("morton", "tile"), None, None),
        ),
        out_specs=(P(("morton", "tile"), None, None), P(("morton", "tile"), None, None)),
        check_vma=False,
    )
```

```python
import functools

import jax
import jax.numpy as jnp
from jax import lax
from jax.experimental import pallas as pl
from jax.experimental.pallas import tpu as pltpu
from jax.sharding import PartitionSpec as P

SCALE = 0.2
REACH = 64.0
GEN = 8
USE = 8
LAG = 3
CUT = 32
ROWS = 16
VMEM = 50 * 2**20


def pick_places(index_ref, pos_ref, out_ref, pos32):
    axes, _, blk = pos_ref.shape
    pos32[...] = pos_ref[...].astype(jnp.float32)
    for q in range(out_ref.shape[0]):
        lines = {}
        for c in range(index_ref.shape[0]):
            for n in range(axes):
                line = pos32[n, pl.ds(index_ref[c, q], 1), :]
                lines[c * axes + n] = jnp.broadcast_to(line, (8, blk))
        out_ref[q] = rows_of(lines, (8, blk)).astype(out_ref.dtype)


def pick_moments(index_ref, count_ref, m_ref, out_ref):
    def one(q, carry):
        for c in range(index_ref.shape[0]):
            kept = jnp.where(count_ref[q] > c, m_ref[index_ref[c, q]].astype(jnp.float32), 0.0)
            out_ref[q, c] = kept.astype(out_ref.dtype)
        return carry

    lax.fori_loop(0, index_ref.shape[1], one, 0, unroll=8)


def picked(kernel, scalars, table, out_shape, scratch, name):
    return pl.pallas_call(
        kernel,
        grid_spec=pltpu.PrefetchScalarGridSpec(
            num_scalar_prefetch=len(scalars),
            grid=(1,),
            in_specs=[pl.BlockSpec(table.shape, lambda g, *_: (0,) * table.ndim)],
            out_specs=pl.BlockSpec(out_shape, lambda g, *_: (0,) * len(out_shape)),
            scratch_shapes=scratch,
        ),
        out_shape=jax.ShapeDtypeStruct(out_shape, table.dtype),
        compiler_params=pltpu.CompilerParams(vmem_limit_bytes=60 * 2**20),
        cost_estimate=pl.CostEstimate(flops=0, bytes_accessed=1024, transcendentals=0),
        name=name,
    )(*scalars, table)


def squares(x, y, z):
    x, y, z = x * x, y * y, z * z
    return x + y + z, 2.0 * z - x - y


def pieces(value):
    high = value.astype(jnp.bfloat16).astype(jnp.float32)
    rest = value - high
    middle = rest.astype(jnp.bfloat16).astype(jnp.float32)
    return high, middle, rest - middle


def rows_of(table, shape):
    row = lax.broadcasted_iota(jnp.int32, shape, 0)
    out = jnp.zeros(shape, jnp.float32)
    for at, value in table.items():
        out = jnp.where(row == at, value, out)
    return out


def reading_features(read_ref, feat_ref, far_ref):
    x, y, z = (read_ref[c].astype(jnp.float32) for c in range(3))
    close, tilt = squares(x, y, z)
    lines = [x, y, z, *pieces(close), *pieces(tilt)]
    shape = (8, x.shape[1])
    size = jnp.maximum(jnp.maximum(jnp.abs(x), jnp.abs(y)), jnp.abs(z))
    far = functools.reduce(jnp.maximum, [size[r : r + 8] for r in range(0, size.shape[0], 8)])
    first = pl.program_id(0) == 0
    far_ref[...] = jnp.maximum(jnp.where(first, 0.0, far_ref[...]), far)
    for b in range(feat_ref.shape[0]):
        line = [jnp.broadcast_to(v[b : b + 1], shape) for v in lines]
        top = rows_of(dict(enumerate(line[:8])), shape)
        low = rows_of({0: line[8], 1: 1.0, 2: 1.0, 3: 1.0}, shape)
        feat_ref[b] = jnp.transpose(jnp.concatenate([top, low], 0)).astype(feat_ref.dtype)


def features(reading_pos):
    axes, rb, blk = reading_pos.shape
    return pl.pallas_call(
        reading_features,
        grid=(rb // 16,),
        in_specs=[pl.BlockSpec((axes, 16, blk), lambda g: (0, g, 0))],
        out_specs=[
            pl.BlockSpec((16, blk, ROWS), lambda g: (g, 0, 0)),
            pl.BlockSpec((8, blk), lambda g: (0, 0)),
        ],
        out_shape=[
            jax.ShapeDtypeStruct((rb, blk, ROWS), jnp.bfloat16),
            jax.ShapeDtypeStruct((8, blk), jnp.float32),
        ],
        compiler_params=pltpu.CompilerParams(vmem_limit_bytes=VMEM),
        cost_estimate=pl.CostEstimate(
            flops=0, bytes_accessed=4 * rb * blk * blk, transcendentals=0
        ),
        name="features",
    )(reading_pos)


def make_kernels(cols_ref, pos_ref, far_ref, feat_ref, out_ref, weight_ref, fits_ref):
    group, blk, wide = out_ref.shape
    near = wide // blk
    axes = 3
    step = pl.program_id(0)
    first = step * group

    @pl.when(step == 0)
    def _():
        far = jnp.maximum(
            jnp.max(jnp.abs(pos_ref[...].astype(jnp.float32))), jnp.max(far_ref[...])
        )
        fits_ref[0] = (far <= REACH).astype(jnp.int32)
        shape = (8, blk)

        def prepare(q, carry):
            p = pos_ref[q].astype(jnp.float32)
            for c in range(2):
                x, y, z = (
                    jnp.broadcast_to(p[c * axes + n : c * axes + n + 1], shape) for n in range(axes)
                )
                close, tilt = squares(x, y, z)
                a, t = pieces(close), pieces(tilt)
                lines = (
                    {0: -2.0 * x, 1: -2.0 * y, 2: -2.0 * z, 3: 1.0, 4: 1.0, 5: 1.0},
                    {1: a[0], 2: a[1], 3: a[2]},
                    {0: 2.0 * x, 1: 2.0 * y, 2: -4.0 * z, 6: 1.0, 7: 1.0},
                    {0: 1.0, 1: t[0], 2: t[1], 3: t[2]},
                )
                part = [rows_of(line, shape) for line in lines]
                left = jnp.concatenate(part[:2], 0)
                right = jnp.concatenate(part[2:], 0)
                both = jnp.concatenate([left, right], 1)
                weight_ref[2 * q + c] = both.astype(weight_ref.dtype)
            return carry

        lax.fori_loop(0, pos_ref.shape[0], prepare, 0, unroll=2)

    fits = fits_ref[0] > 0

    @pl.when(fits)
    def _():
        for b in range(group):
            for k in range(0, near, 2):
                both = [
                    jnp.dot(
                        feat_ref[b],
                        weight_ref[cols_ref[k + c, first + b]],
                        preferred_element_type=jnp.float32,
                    )
                    for c in range(2)
                ]
                for r in range(0, blk, 8):
                    pair = []
                    for part in both:
                        inv = lax.rsqrt(part[r : r + 8, :blk])
                        inv2 = inv * inv
                        pair.append((SCALE * part[r : r + 8, blk:]) * (inv2 * inv2) * inv)
                    out_ref[b, r : r + 8, k * blk : (k + 2) * blk] = jnp.concatenate(
                        pair, 1
                    ).astype(out_ref.dtype)

    @pl.when(jnp.logical_not(fits))
    def _():
        def one_reading(b, carry):
            place = feat_ref[b].astype(jnp.float32)
            rx, ry, rz = (
                jnp.broadcast_to(place[:, c : c + 1], (blk, blk)) for c in range(axes)
            )

            def one_block(k, carry):
                s = cols_ref[k, first + b]
                p = pos_ref[lax.div(s, 2)].astype(jnp.float32)
                odd = lax.rem(s, 2) > 0
                px, py, pz = (
                    jnp.where(odd, p[axes + c : axes + c + 1], p[c : c + 1]) for c in range(axes)
                )
                dx, dy, dz = rx - px, ry - py, rz - pz
                flat, up = dx * dx + dy * dy, dz * dz
                inv = lax.rsqrt(flat + up)
                inv2 = inv * inv
                value = (SCALE * (up + up - flat)) * (inv2 * inv2) * inv
                out_ref[b, :, pl.ds(pl.multiple_of(k * blk, blk), blk)] = value.astype(
                    out_ref.dtype
                )
                return carry

            return lax.fori_loop(0, near, one_block, carry)

        lax.fori_loop(0, group, one_reading, 0)


def kernel_values(near_cols, slot_p, far, feat):
    rb, blk, _ = feat.shape
    near = near_cols.shape[0]
    whole = lambda g, *_: (0, 0, 0)
    part = lambda g, *_: (g, 0, 0)
    return pl.pallas_call(
        make_kernels,
        grid_spec=pltpu.PrefetchScalarGridSpec(
            num_scalar_prefetch=1,
            grid=(rb // GEN,),
            in_specs=[
                pl.BlockSpec(slot_p.shape, whole),
                pl.BlockSpec(far.shape, lambda g, *_: (0, 0)),
                pl.BlockSpec((GEN, blk, ROWS), part),
            ],
            out_specs=pl.BlockSpec((GEN, blk, near * blk), part),
            scratch_shapes=[
                pltpu.VMEM((2 * slot_p.shape[0], ROWS, 2 * blk), jnp.bfloat16),
                pltpu.SMEM((1,), jnp.int32),
            ],
        ),
        out_shape=jax.ShapeDtypeStruct((rb, blk, near * blk), jnp.bfloat16),
        compiler_params=pltpu.CompilerParams(vmem_limit_bytes=VMEM),
        cost_estimate=pl.CostEstimate(
            flops=15 * rb * near * blk * blk,
            bytes_accessed=2 * rb * near * blk * blk,
            transcendentals=rb * near * blk * blk,
        ),
        name="kernel_values",
    )(near_cols, slot_p, far, feat)


def apply_both(cols_ref, slot_ref, me_ref, kern_ref, m_ref, *refs):
    *seen_refs, field_ref, adj_ref, total, obs_ref = refs
    group, blk, wide = kern_ref.shape
    near = wide // blk
    step = pl.program_id(0)
    tiles, rb, me = len(seen_refs), obs_ref.shape[0], me_ref[0]
    share = rb // tiles

    @pl.when(step == 0)
    def _():
        total[...] = jnp.zeros_like(total)
        for n, ref in enumerate(seen_refs):
            obs_ref[n * share : (n + 1) * share] = ref[...]

    def forward(b):
        i = step * group + b
        field = None
        for k in range(0, near, 2):
            part = lax.dot_general(
                jnp.concatenate([m_ref[cols_ref[k, i]], m_ref[cols_ref[k + 1, i]]], 1),
                kern_ref[b, :, k * blk : (k + 2) * blk],
                (((1,), (1,)), ((), ())),
                preferred_element_type=jnp.float32,
            )
            field = part if field is None else field + part
        field = field.astype(jnp.bfloat16)
        there = lax.div(slot_ref[i], rb)
        within = lax.rem(slot_ref[i], share)
        field_ref[lax.rem(there + tiles - me, tiles) * share + within] = field
        row = lax.rem(me + tiles - there, tiles) * share + within
        seen = obs_ref[row].astype(jnp.float32)
        return (field.astype(jnp.float32) - seen).astype(jnp.bfloat16)

    def adjoint(b, residual):
        i = step * group + b
        for k in range(0, near, 2):
            both = jnp.dot(
                residual,
                kern_ref[b, :, k * blk : (k + 2) * blk],
                preferred_element_type=jnp.float32,
            )
            total[cols_ref[k, i]] += both[:, :blk]
            total[cols_ref[k + 1, i]] += both[:, blk:]

    residuals = []
    for b in range(group):
        residuals.append(forward(b))
        if b >= LAG:
            adjoint(b - LAG, residuals[b - LAG])
    for b in range(group - LAG, group):
        adjoint(b, residuals[b])

    @pl.when(step == pl.num_programs(0) - 1)
    def _():
        adj_ref[...] = total[...].astype(adj_ref.dtype)


def forward_adjoint(near_cols, grid_slot, me, kern, slot_m, seen):
    rb, blk, wide = kern.shape
    slots, width, _ = slot_m.shape
    whole = lambda g, *_: (0, 0, 0)
    return pl.pallas_call(
        apply_both,
        grid_spec=pltpu.PrefetchScalarGridSpec(
            num_scalar_prefetch=3,
            grid=(rb // USE,),
            in_specs=[
                pl.BlockSpec((USE, blk, wide), lambda g, *_: (g, 0, 0)),
                pl.BlockSpec(slot_m.shape, whole),
                *[pl.BlockSpec(part.shape, whole) for part in seen],
            ],
            out_specs=[pl.BlockSpec((rb, width, blk), whole), pl.BlockSpec((slots, width, blk), whole)],
            scratch_shapes=[
                pltpu.VMEM((slots, width, blk), jnp.float32),
                pltpu.VMEM((rb, width, blk), jnp.bfloat16),
            ],
        ),
        out_shape=[
            jax.ShapeDtypeStruct((rb, width, blk), jnp.bfloat16),
            jax.ShapeDtypeStruct((slots, width, blk), jnp.bfloat16),
        ],
        compiler_params=pltpu.CompilerParams(vmem_limit_bytes=VMEM),
        cost_estimate=pl.CostEstimate(
            flops=4 * width * rb * wide * blk, bytes_accessed=2 * rb * wide * blk, transcendentals=0
        ),
        name="forward_adjoint",
    )(near_cols, grid_slot, me, kern, slot_m, *seen)


def shift(block, axis, by, size):
    return lax.ppermute(block, axis, [(i, (i + by) % size) for i in range(size)])


def add_back(index_ref, count_ref, back_ref, out_ref):
    out_ref[...] = jnp.zeros_like(out_ref)

    def one(q, carry):
        for c in range(back_ref.shape[1]):
            value = back_ref[q, c].astype(jnp.float32)
            out_ref[index_ref[c, q]] += jnp.where(count_ref[q] > c, value, 0.0)
        return carry

    lax.fori_loop(0, back_ref.shape[0], one, 0, unroll=2)


def combine(send_index, send_count, back, old):
    _, _, width, depth = back.shape
    return pl.pallas_call(
        add_back,
        grid_spec=pltpu.PrefetchScalarGridSpec(
            num_scalar_prefetch=2,
            grid=(width // CUT,),
            in_specs=[pl.BlockSpec((*back.shape[:2], CUT, depth), lambda g, *_: (0, 0, g, 0))],
            out_specs=pl.BlockSpec((old, CUT, depth), lambda g, *_: (0, g, 0)),
        ),
        out_shape=jax.ShapeDtypeStruct((old, width, depth), jnp.float32),
        compiler_params=pltpu.CompilerParams(vmem_limit_bytes=VMEM),
        name="combine",
    )(send_index, send_count, back)


def on_device(
    moments, dipole_pos, send_index, send_count, reading_pos, near_cols, grid_slot, observed
):
    peers = lax.axis_size("morton")
    tiles = lax.axis_size("tile")
    cap = send_index.shape[1]
    old, width, depth = moments.shape
    rb = reading_pos.shape[0]
    share = rb // tiles
    swap = functools.partial(lax.all_to_all, split_axis=0, concat_axis=0, tiled=True)
    send_index, near_cols = send_index.T, near_cols.T
    dipole_pos, reading_pos = (jnp.swapaxes(a, 0, 1) for a in (dipole_pos, reading_pos))
    send_p = picked(
        pick_places,
        (send_index,),
        dipole_pos,
        (peers, 8, depth),
        [pltpu.VMEM(dipole_pos.shape, jnp.float32)],
        "pick_places",
    )
    send_m = picked(
        pick_moments,
        (send_index, send_count),
        moments,
        (peers, cap, width, depth),
        [],
        "pick_moments",
    )
    slot_p = swap(send_p, "morton")
    feat, far = features(reading_pos)
    feat, observed = lax.optimization_barrier((feat, observed))
    me = lax.axis_index("tile")
    seen = [
        lax.dynamic_slice_in_dim(observed, (me + by) % tiles * share, share, 0)
        for by in range(tiles)
    ]
    slot_p, *seen = lax.optimization_barrier((slot_p, *seen))
    send_m, feat, *seen = lax.optimization_barrier((send_m, feat, *seen))
    seen = [shift(part, "tile", by, tiles) if by else part for by, part in enumerate(seen)]
    slot_m = swap(send_m, "morton").reshape(peers * cap, width, depth)
    kern = kernel_values(near_cols, slot_p, far, feat)
    ordered, slot_adj = forward_adjoint(near_cols, grid_slot, me.reshape(1), kern, slot_m, seen)
    back = swap(slot_adj.reshape(peers, cap, width, depth), "morton")
    field = jnp.zeros_like(ordered)
    for by in range(tiles):
        part = ordered[by * share : (by + 1) * share]
        part = shift(part, "tile", by, tiles) if by else part
        field = lax.dynamic_update_slice_in_dim(field, part, (me - by) % tiles * share, 0)
    adjoint_moments = combine(send_index, send_count, back, old)
    return (field, adjoint_moments)


def solution(mesh):
    return jax.shard_map(
        on_device,
        mesh=mesh,
        in_specs=(
            P(("morton", "tile"), None, None),
            P(("morton", "tile"), None, None),
            P(("morton", "tile"), None),
            P(("morton", "tile")),
            P(("morton", "tile"), None, None),
            P(("morton", "tile"), None),
            P(("morton", "tile")),
            P(("morton", "tile"), None, None),
        ),
        out_specs=(P(("morton", "tile"), None, None), P(("morton", "tile"), None, None)),
        check_vma=False,
    )
```
